512 devices in a mesh: seg: 16 (over z, core), dev: 32 (over y, x).
Axes of the slice: x: 4, y: 8, z: 8, core: 2. Of those that a mesh axis runs over, the one named last changes fastest.
Arguments:
- positions: float32 [3, 16, 12288, 128], P(None, 'seg', 'dev'), may hold values from -6 to 6
- velocity: float32 [3, 16, 12288, 128], P(None, 'seg', 'dev'), may hold values from -6 to 6
- node_mass: bfloat16 [16, 12288, 128], P('seg', 'dev'), may hold values from 0.5 to 2
- stiffness: bfloat16 [16, 12288, 128], P('seg', 'dev'), may hold values from 0.25 to 2
- contact_patch: int32 [16, 32, 32], P('seg', 'dev'), may hold values from -1 to 2, as said below
- cross_patch: int32 [16, 32, 2], P('seg', 'dev'), may hold values from 0 to 2
Outputs:
- velocity_next: float32 [3, 16, 12288, 128], P(None, 'seg', 'dev')
The draws below stay inside these ranges and needn't reach their ends.
Inputs may be any that keep to these rules, and one draw needn't show every extreme that they name: `contact_patch`: entry [s, i, q] is -1 where runs i and q of segment s form no contact pair, else the number within run i of run i's patch in that pair; entry [s, i, q] is -1 exactly when entry [s, q, i] is; entries [s, i, i] are -1; in every segment some run has a pair with every other run. `cross_patch`: entry [s, i, 0] is the number within run i of the patch of segment s that meets run i of the next segment; entry [s, i, 1] the one that meets run i of the previous segment.
All inputs are finite; a program needn't handle non-finite values.
Results may differ from the reference program's by a relative error of at most 0.0028.
Values may be sent and summed in bfloat16 or wider, within the bound.
A program may use at most 64 MiB of HBM per device.

```python
import math
import jax
import jax.numpy as jnp
import numpy as np
from jax import lax

P_DEV = 3
PATCH_ROWS = 128
COLS = 128
BAND = 4
SEGS = 16
RUNS = 32
STRIP = 12288


def draw_contact_patch(key, part):
    base = jax.random.fold_in(key, 7)
    key_links, key_hub, key_patch = jax.random.split(base, 3)
    coins = (jax.random.randint(key_links, (SEGS, RUNS, RUNS), 0, 5) >= 1).astype(jnp.int32)
    upper = jnp.triu(coins, 1)
    linked = upper + jnp.swapaxes(upper, 1, 2) > 0
    hub_run = jax.random.randint(key_hub, (SEGS, 1, 1), 0, RUNS)
    ranks = jnp.arange(RUNS)
    touching = (ranks[None, :, None] == hub_run) | (ranks[None, None, :] == hub_run)
    apart = ranks[:, None] != ranks[None, :]
    linked = (linked | touching) & apart[None]
    chosen = jax.random.randint(key_patch, (SEGS, RUNS, RUNS), 0, P_DEV)
    return jnp.where(linked, chosen, -1).astype(jnp.int32)


def set_ends(values, stream_key, smallest, high):
    place = [jax.random.randint(jax.random.fold_in(stream_key, axis), (), 0, length) for axis, length in enumerate(values.shape)]
    main_axis = values.shape.index(max(values.shape))
    neighbour = place[:main_axis] + [(place[main_axis] + 1) % values.shape[main_axis]] + place[main_axis + 1:]
    return values.at[tuple(place)].set(smallest).at[tuple(neighbour)].set(high)


def block_scale(stream_key, shape, shards, low, high):
    def one(dim, parts):
        steps = jax.random.uniform(jax.random.fold_in(jax.random.fold_in(stream_key, 6), dim), (parts,), jnp.float32, low / len(shards), high / len(shards))
        return jnp.repeat(jnp.exp(steps), shape[dim] // parts).reshape((-1,) + (1,) * (len(shape) - dim - 1))

    level = one(*shards[0])
    for cut in shards[1:]:
        level = level * one(*cut)
    return level


def normal_values(key, shape, scale, limit, cuts=(), held_as=jnp.bfloat16):
    drawn = scale * jax.random.normal(key, shape, jnp.float32)
    if cuts:
        drawn = drawn * block_scale(key, shape, cuts, -0.22, 0.18)
    return jnp.clip(drawn, -limit, limit).astype(held_as)


def setup_inputs(seed: int = 0) -> dict:
    keys = jax.random.split(jax.random.key(seed), 7)
    return {
        "positions": normal_values(keys[0], (3, SEGS, STRIP, COLS), 1.0, 6.0, ((1, 16), (2, 32)), jnp.float32),
        "velocity": normal_values(keys[1], (3, SEGS, STRIP, COLS), 1.0, 6.0, ((1, 16), (2, 32)), jnp.float32),
        "node_mass": jnp.clip(jnp.exp(math.log(2.0) - 1.3862944 * jax.random.uniform(keys[2], (SEGS, STRIP, COLS), jnp.float32) ** block_scale(keys[2], (SEGS, STRIP, COLS), ((0, 16), (1, 32)), -0.2, 0.2)), 0.5, 2.0).astype(jnp.bfloat16),
        "stiffness": jnp.clip(jnp.exp(math.log(2.0) - 2.0794415 * jax.random.uniform(keys[3], (SEGS, STRIP, COLS), jnp.float32) ** block_scale(keys[3], (SEGS, STRIP, COLS), ((0, 16), (1, 32)), -0.2, 0.2)), 0.25, 2.0).astype(jnp.bfloat16),
        "contact_patch": draw_contact_patch(jax.random.fold_in(keys[6], 71), 0),
        "cross_patch": set_ends(jax.random.randint(keys[5], (SEGS, RUNS, 2), 0, P_DEV), jax.random.fold_in(keys[5], 1), 0, P_DEV - 1).astype(jnp.int32),
    }


penalty = 1.5
reach_sq = 4.0
time_step = 0.2


def pair_forces(own_patch, other_patch):
    columns = own_patch.shape[-1]
    leading = [(0, 0)] * (own_patch.ndim - 1)
    padded = jnp.pad(other_patch, leading + [(BAND, BAND)])
    inside = jnp.pad(jnp.ones((columns,), jnp.float32), (BAND, BAND))
    force_own = jnp.zeros(own_patch.shape, jnp.float32)
    force_other = jnp.zeros(padded.shape, jnp.float32)
    for offset in range(2 * BAND + 1):
        facing = padded[..., offset:offset + columns]
        differ = own_patch - facing
        weight = penalty * jnp.exp(-jnp.sum(differ * differ, axis=-3, keepdims=True) / reach_sq) * inside[offset:offset + columns]
        pulled = weight * differ
        force_own = force_own + pulled
        force_other = force_other - jnp.pad(pulled, leading + [(offset, 2 * BAND - offset)])
    return force_own, force_other[..., BAND:BAND + columns]


def internal_force(positions, springs):
    still = (0, 0)
    row_flow = 0.5 * (springs[:, 1:] + springs[:, :-1]) * (positions[:, :, 1:] - positions[:, :, :-1])
    col_flow = 0.5 * (springs[:, :, 1:] + springs[:, :, :-1]) * (positions[..., 1:] - positions[..., :-1])
    total = jnp.pad(row_flow, (still, still, (0, 1), still)) - jnp.pad(row_flow, (still, still, (1, 0), still))
    total = total + jnp.pad(col_flow, (still, still, still, (0, 1))) - jnp.pad(col_flow, (still, still, still, (1, 0)))
    return total


def reference(positions, velocity, node_mass, stiffness, contact_patch, cross_patch):
    internal = internal_force(positions, stiffness.astype(jnp.float32))
    rounded = lax.optimization_barrier(positions.astype(jnp.bfloat16)).astype(jnp.float32)
    low_np, high_np = np.triu_indices(RUNS, 1)
    paired = len(low_np)
    seg_pairs = jnp.asarray(np.repeat(np.arange(SEGS), paired), dtype=jnp.int32)
    run_low = jnp.asarray(np.tile(low_np, SEGS), dtype=jnp.int32)
    run_high = jnp.asarray(np.tile(high_np, SEGS), dtype=jnp.int32)
    entry_low = contact_patch[seg_pairs, run_low, run_high]
    entry_high = contact_patch[seg_pairs, run_high, run_low]
    live_pairs = (entry_low >= 0).astype(jnp.float32)
    row_low = (run_low * P_DEV + jnp.maximum(entry_low, 0)) * PATCH_ROWS
    row_high = (run_high * P_DEV + jnp.maximum(entry_high, 0)) * PATCH_ROWS
    cross_seg = jnp.asarray(np.repeat(np.arange(SEGS), RUNS), dtype=jnp.int32)
    cross_run = jnp.asarray(np.tile(np.arange(RUNS), SEGS), dtype=jnp.int32)
    next_seg = (cross_seg + 1) % SEGS
    cross_low = (cross_run * P_DEV + cross_patch[cross_seg, cross_run, 0]) * PATCH_ROWS
    cross_high = (cross_run * P_DEV + cross_patch[next_seg, cross_run, 1]) * PATCH_ROWS
    items = (jnp.concatenate([seg_pairs, cross_seg]).astype(jnp.int32),
             jnp.concatenate([row_low, cross_low]).astype(jnp.int32),
             jnp.concatenate([seg_pairs, next_seg]).astype(jnp.int32),
             jnp.concatenate([row_high, cross_high]).astype(jnp.int32),
             jnp.concatenate([live_pairs, jnp.ones((SEGS * RUNS,), jnp.float32)]))
    extent = (3, 1, PATCH_ROWS, COLS)

    def visit(contact, item):
        seg_low, start_row_low, seg_high, start_row_high, live = item
        zero = jnp.zeros((), jnp.int32)
        start_low = (zero, seg_low, start_row_low, zero)
        start_high = (zero, seg_high, start_row_high, zero)
        low_patch = lax.dynamic_slice(rounded, start_low, extent)[:, 0]
        high_patch = lax.dynamic_slice(rounded, start_high, extent)[:, 0]
        force_low, force_high = pair_forces(low_patch, high_patch)
        current = lax.dynamic_slice(contact, start_low, extent)
        contact = lax.dynamic_update_slice(contact, current + live * force_low[:, None], start_low)
        current = lax.dynamic_slice(contact, start_high, extent)
        contact = lax.dynamic_update_slice(contact, current + live * force_high[:, None], start_high)
        return contact, None

    contact, _ = lax.scan(visit, jnp.zeros(positions.shape, jnp.float32), items)
    return velocity + time_step * (internal + contact) / node_mass.astype(jnp.float32)
```

```python
import functools
import math

import jax
import jax.numpy as jnp
from jax import lax
from jax.experimental import pallas as pl
from jax.experimental.pallas import tpu as pltpu
from jax.sharding import PartitionSpec as P

RUNS = 32
XS = 4
YS = 8
PATCHES = 3
N = 128
BAND = 4
PAD = 8
STRIDE = 4
WINDOW = 8 * STRIDE
ROWS = PATCHES * N

penalty = 1.5
reach_sq = 4.0
time_step = 0.2
K = math.log2(math.e) / reach_sq
FAR = -1.0e4

CHUNKS = ((0, 80, (0, 1)), (80, 128, (2, 3)))
OPPOSITE = (((0, 48), (48, 80)), ((80, 96), (96, 128)))
HALVES = OPPOSITE

TWO, RIGHT, LEFT, OWN = range(4)
COPIES = 160


class Copies:
    def __init__(self, send_sem, recv_sem):
        self.send_sem, self.recv_sem = send_sem, recv_sem
        self.made = {}

    def start(self, name, src, dst, device):
        n = len(self.made)
        copy = pltpu.make_async_remote_copy(
            src_ref=src,
            dst_ref=dst,
            send_sem=self.send_sem.at[n],
            recv_sem=self.recv_sem.at[n],
            device_id=device,
            device_id_type=pl.DeviceIdType.MESH,
        )
        copy.start()
        self.made[name] = copy

    def arrived(self, name):
        self.made[name].wait_recv()

    def sent(self):
        for copy in self.made.values():
            copy.wait_send()


def kernel(
    table, cross, pos, vel, mass, stiff, out,
    place, mass_v, stiff_v, spring, share, own, y_land, x_land, src, tgt, acc,
    ship, raw, done, force, z_send, z_land, h_send, h_land,
    tab_y1, tab_y2, tab_y3, tab_y4, tab_y5, tab_y6, tab_y7, tab_x1, tab_x2, tab_x3, pick,
    local_sem, send_sem, recv_sem,
):
    seg = lax.axis_index("seg")
    dev = lax.axis_index("dev")
    segs = lax.axis_size("seg")
    y = dev // XS
    x = dev % XS

    def at(dy, dx):
        return (seg, lax.rem(y + dy, YS) * XS + lax.rem(x + dx, XS))

    up, down = at(1, 0), at(YS - 1, 0)
    right, left = at(0, 1), at(0, XS - 1)
    seg_next, seg_prev = (lax.rem(seg + 1, segs), dev), (lax.rem(seg + segs - 1, segs), dev)
    dev_next, dev_prev = (seg, lax.rem(dev + 1, RUNS)), (seg, lax.rem(dev + RUNS - 1, RUNS))

    barrier = pltpu.get_barrier_semaphore()
    peers = (up, down, right, left, seg_next, seg_prev, dev_next, dev_prev)
    for peer in peers:
        pl.semaphore_signal(barrier, inc=1, device_id=peer, device_id_type=pl.DeviceIdType.MESH)

    loads = []
    for p in range(PATCHES):
        loads.append(
            pltpu.make_async_copy(
                pos.at[:, 0, pl.ds(p * N, N), :],
                place.at[:, pl.ds(PAD + p * N, N), :],
                local_sem.at[p],
            )
        )
    loads.append(pltpu.make_async_copy(stiff.at[0], stiff_v, local_sem.at[3]))
    loads.append(pltpu.make_async_copy(mass.at[0], mass_v, local_sem.at[4]))
    loads.append(pltpu.make_async_copy(vel, out, local_sem.at[5]))
    for load in loads:
        load.start()

    def clear(n, carry):
        for c in range(4):
            edge = jnp.full((PAD, N), FAR if c == 3 else 0.0, jnp.float32)
            src[n, c, pl.ds(0, PAD), :] = edge
            src[n, c, pl.ds(PAD + N, PAD), :] = edge
        return carry

    lax.fori_loop(0, 8 * PATCHES + 2, clear, 0)

    copies = Copies(send_sem, recv_sem)

    def columns(k):
        lo, hi, _ = CHUNKS[k]
        return pl.ds(lo, hi - lo)

    def beta(xs):
        return -K * (xs[0] * xs[0] + xs[1] * xs[1] + xs[2] * xs[2])

    entered = False
    for p in range(PATCHES):
        loads[p].wait()
        parts = []
        for c in range(3):
            turned = place[c, pl.ds(PAD + p * N, N), :].T.astype(jnp.bfloat16)
            own[p, c] = turned
            parts.append(turned.astype(jnp.float32))
        for c in range(3):
            src[p, c, pl.ds(PAD, N), :] = parts[c]
            tgt[OWN * PATCHES + p, c] = parts[c] * (2 * K)
        src[p, 3, pl.ds(PAD, N), :] = beta(parts)
        if not entered:
            pl.semaphore_wait(barrier, len(peers))
            entered = True
        part = own.at[p, :, columns(0), :]
        copies.start(("y", 1, 0, p), part, y_land.at[0, p, :, columns(0), :], up)
        copies.start(("y", -1, 0, p), part, y_land.at[3, p, :, columns(0), :], down)
        copies.start(("x", 1, 0, p), part, x_land.at[LEFT, p, :, columns(0), :], right)
        copies.start(("x", -1, 0, p), part, x_land.at[RIGHT, p, :, columns(0), :], left)
    tabs_y = (table, tab_y1, tab_y2, tab_y3, tab_y4, tab_y5, tab_y6, tab_y7)
    copies.start(("ty", 1), table, tab_y1, up)
    copies.start(("ty", -1), table, tab_y4, down)
    copies.start(("tx", 1), table, tab_x3, right)
    copies.start(("tx", -1), table, tab_x2, left)
    for p in range(PATCHES):
        part = own.at[p, :, columns(1), :]
        copies.start(("y", 1, 1, p), part, y_land.at[0, p, :, columns(1), :], up)
        copies.start(("y", -1, 1, p), part, y_land.at[3, p, :, columns(1), :], down)
    meets = [cross[0, 0], cross[0, 1]]
    for c in range(3):
        z_send[0, c] = own[meets[0], c]
        z_send[1, c] = own[meets[1], c]
    copies.start(("z", 1), z_send.at[0], z_land.at[1], seg_next)
    copies.start(("z", -1), z_send.at[1], z_land.at[0], seg_prev)

    loads[3].wait()
    for b in range(ROWS // WINDOW):
        spring[pl.ds(PAD + b * WINDOW, WINDOW), :] = stiff_v[pl.ds(b * WINDOW, WINDOW), :].astype(jnp.float32)
    for e, row in enumerate((PAD, PAD + ROWS - 1)):
        for c in range(3):
            h_send[e, pl.ds(c, 1), :] = place[c, pl.ds(row, 1), :]
        h_send[e, pl.ds(3, 1), :] = spring[pl.ds(row, 1), :]
        h_send[e, pl.ds(4, 4), :] = jnp.zeros((4, N), jnp.float32)
    copies.start(("h", -1), h_send.at[0], h_land.at[1], dev_prev)
    copies.start(("h", 1), h_send.at[1], h_land.at[0], dev_next)

    def clear_sums(n, carry):
        for c in range(4):
            acc[n, c] = jnp.zeros((N, N), jnp.float32)
        return carry

    lax.fori_loop(0, 4 * PATCHES, clear_sums, 0)

    def interact(i, ia, sb, w):
        sa = i * PATCHES + jnp.maximum(ia, 0)
        base = w * WINDOW
        seen = {}

        def b(j, c):
            if (j, c) not in seen:
                seen[j, c] = src[sb, c, pl.ds(base + (PAD + j), 8, stride=STRIDE), :]
            return seen[j, c]

        for u in range(STRIDE):
            a = [tgt[sa, c, pl.ds(base + u, 8, stride=STRIDE), :] for c in range(3)]
            sums = [None] * 4
            for t in range(-BAND, BAND + 1):
                bs = [b(u + t, c) for c in range(4)]
                w_ = jnp.exp2((a[0] * bs[0] + a[1] * bs[1]) + (a[2] * bs[2] + bs[3]))
                terms = [w_ * bs[0], w_ * bs[1], w_ * bs[2], w_]
                sums = [g if s is None else s + g for s, g in zip(sums, terms)]
            rows = pl.ds(pl.multiple_of(base + u * 8, 8), 8)
            for p in range(PATCHES):
                for c in range(4):
                    acc[i * PATCHES + p, c, rows, :] += jnp.where(ia == p, sums[c], 0.0)

    def sources(q, land, k):
        lo, hi, _ = CHUNKS[k]

        def one(p, carry):
            parts = [land[p, c, pl.ds(lo, hi - lo), :].astype(jnp.float32) for c in range(3)]
            for c in range(3):
                src[q * PATCHES + p, c, pl.ds(PAD + lo, hi - lo), :] = parts[c]
            src[q * PATCHES + p, 3, pl.ds(PAD + lo, hi - lo), :] = beta(parts)
            return carry

        lax.fori_loop(0, PATCHES, one, 0)

    def targets(i, k):
        lo, hi, _ = CHUNKS[k]

        def one(p, carry):
            for c in range(3):
                part = x_land[i, p, c, pl.ds(lo, hi - lo), :].astype(jnp.float32)
                tgt[i * PATCHES + p, c, pl.ds(lo, hi - lo), :] = part * (2 * K)
            return carry

        lax.fori_loop(0, PATCHES, one, 0)

    tabs_x = (tab_x1, tab_x2, tab_x3, table)
    run_y = [lax.rem(y + d, YS) for d in (0, 7, 6, 5, 1, 2, 3, 4)]
    run_x = [lax.rem(x + d, XS) for d in (2, 1, 3, 0)]

    def choose(q, i):
        pick[0, q * 4 + i] = tabs_x[i][0, run_y[q] * XS + x]
        pick[1, q * 4 + i] = q * PATCHES + jnp.maximum(tabs_y[q][0, y * XS + run_x[i]], 0)

    def meet(q, k, first, last):
        w0 = CHUNKS[k][2][0]

        def one(n, carry):
            i = first + n // 2
            interact(i, pick[0, q * 4 + i], pick[1, q * 4 + i], w0 + n % 2)
            return carry

        lax.fori_loop(0, 2 * (last - first), one, 0)

    def reduced(i, w, u, p):
        rows = pl.ds(w * WINDOW + u * 8, 8)
        a = [tgt[i * PATCHES + p, c, pl.ds(w * WINDOW + u, 8, stride=STRIDE), :] for c in range(3)]
        level = penalty * jnp.exp2((a[0] * a[0] + a[1] * a[1] + a[2] * a[2]) * (-0.25 / K))
        whole = acc[i * PATCHES + p, 3, rows, :] * (0.5 / K)
        return [level * (a[c] * whole - acc[i * PATCHES + p, c, rows, :]) for c in range(3)]

    def pack(i, w, extra=None):
        def one(p, carry):
            for h in range(STRIDE // 2):
                rows = pl.ds(h * 16, 16)
                pair = [reduced(i, w, 2 * h + e, p) for e in range(2)]
                for c in range(3):
                    f = jnp.concatenate([pair[0][c], pair[1][c]], axis=0)
                    if extra is not None:
                        f = f + extra[p, c, rows, :].astype(jnp.float32)
                    ship[i, w, p, c, rows, :] = f.astype(jnp.bfloat16)
            return carry

        lax.fori_loop(0, PATCHES, one, 0)

    def collect(w):
        def one(p, carry):
            for h in range(STRIDE // 2):
                rows = pl.ds(h * 16, 16)
                pair = [reduced(OWN, w, 2 * h + e, p) for e in range(2)]
                for c in range(3):
                    f = jnp.concatenate([pair[0][c], pair[1][c]], axis=0)
                    f = f + done[0, w, p, c, rows, :].astype(jnp.float32)
                    f = f + done[1, w, p, c, rows, :].astype(jnp.float32)
                    for e in range(2):
                        at_rows = pl.ds(w * WINDOW + 2 * h + e, 8, stride=STRIDE)
                        force[p, c, at_rows, :] = f[e * 8 : e * 8 + 8]
            return carry

        lax.fori_loop(0, PATCHES, one, 0)

    def onward(d, k, p):
        for way, slot, peer in ((1, 0, up), (-1, 3, down)):
            copies.arrived(("y", way * (d - 1), k, p))
            if d < 4:
                cols = columns(k)
                to = slot + d - 1
            else:
                lo, hi = OPPOSITE[k][0 if way == 1 else 1]
                cols = pl.ds(lo, hi - lo)
                to = 6
            copies.start(
                ("y", way * d, k, p),
                y_land.at[slot + d - 2, p, :, cols, :],
                y_land.at[to, p, :, cols, :],
                peer,
            )

    def across(k, p):
        for way, slot, peer in ((1, LEFT, right), (-1, RIGHT, left)):
            copies.arrived(("x", way, k, p))
            lo, hi = HALVES[k][0 if way == 1 else 1]
            cols = pl.ds(lo, hi - lo)
            copies.start(
                ("x", 2 * way, k, p),
                x_land.at[slot, p, :, cols, :],
                x_land.at[TWO, p, :, cols, :],
                peer,
            )

    def base_rows(b, carry):
        r = pl.multiple_of(b * 16, 16)
        lane = lax.broadcasted_iota(jnp.int32, (16, N), 1)
        after = jnp.where(lane == N - 1, 0.0, 0.5)
        before = jnp.where(lane == 0, 0.0, 0.5)
        s = spring[pl.ds(PAD + r, 16), :]
        s_up = 0.5 * (s + spring[pl.ds(PAD + r - 1, 16), :])
        s_down = 0.5 * (s + spring[pl.ds(PAD + r + 1, 16), :])
        s_after = after * (s + pltpu.roll(s, N - 1, 1))
        s_before = before * (s + pltpu.roll(s, 1, 1))
        part = time_step / mass_v[pl.ds(r, 16), :].astype(jnp.float32)
        share[pl.ds(r, 16), :] = part
        for c in range(3):
            v = place[c, pl.ds(PAD + r, 16), :]
            f = s_up * (place[c, pl.ds(PAD + r - 1, 16), :] - v)
            f = f + s_down * (place[c, pl.ds(PAD + r + 1, 16), :] - v)
            f = f + s_after * (pltpu.roll(v, N - 1, 1) - v)
            f = f + s_before * (pltpu.roll(v, 1, 1) - v)
            out[c, 0, pl.ds(r, 16), :] = out[c, 0, pl.ds(r, 16), :] + part * f
        return carry

    copies.arrived(("h", -1))
    copies.arrived(("h", 1))
    for e, row, edge, last in ((0, PAD - 1, PAD, 0), (1, PAD + ROWS, PAD + ROWS - 1, RUNS - 1)):
        for c in range(3):
            place[c, pl.ds(row, 1), :] = jnp.where(
                dev == last, place[c, pl.ds(edge, 1), :], h_land[e, pl.ds(c, 1), :]
            )
        spring[pl.ds(row, 1), :] = h_land[e, pl.ds(3, 1), :]
    loads[4].wait()
    loads[5].wait()
    lax.fori_loop(0, ROWS // 16, base_rows, 0)

    for p in range(PATCHES):
        onward(2, 0, p)
        across(0, p)
    for p in range(PATCHES):
        part = own.at[p, :, columns(1), :]
        copies.start(("x", 1, 1, p), part, x_land.at[LEFT, p, :, columns(1), :], right)
        copies.start(("x", -1, 1, p), part, x_land.at[RIGHT, p, :, columns(1), :], left)
    copies.arrived(("ty", 1))
    copies.start(("ty", 2), tab_y1, tab_y2, up)
    copies.arrived(("ty", -1))
    copies.start(("ty", -2), tab_y4, tab_y5, down)
    copies.arrived(("tx", 1))
    copies.start(("tx", 2), tab_x3, tab_x1, right)
    copies.arrived(("tx", -1))
    targets(RIGHT, 0)
    targets(LEFT, 0)
    sources(1, y_land.at[0], 0)
    sources(4, y_land.at[3], 0)
    for q in (0, 1, 4):
        for i in (RIGHT, LEFT, OWN):
            choose(q, i)
    meet(0, 0, RIGHT, OWN)
    meet(1, 0, RIGHT, OWN + 1)
    meet(4, 0, RIGHT, OWN + 1)

    for p in range(PATCHES):
        onward(3, 0, p)
    copies.arrived(("ty", 2))
    copies.start(("ty", 3), tab_y2, tab_y3, up)
    copies.arrived(("ty", -2))
    copies.start(("ty", -3), tab_y5, tab_y6, down)
    copies.arrived(("tx", 2))
    for p in range(PATCHES):
        onward(2, 1, p)
    for p in range(PATCHES):
        across(1, p)
        for way in (2, -2):
            copies.arrived(("x", way, 0, p))
    targets(TWO, 0)
    sources(2, y_land.at[1], 0)
    sources(5, y_land.at[4], 0)
    for q in (0, 1, 4):
        choose(q, TWO)
    for q in (2, 5):
        for i in range(4):
            choose(q, i)
    for q in (0, 1, 4):
        meet(q, 0, TWO, TWO + 1)
    for q in (2, 5):
        meet(q, 0, 0, 4)

    for p in range(PATCHES):
        onward(4, 0, p)
    copies.arrived(("ty", 3))
    copies.start(("ty", 4), tab_y3, tab_y7, up)
    copies.arrived(("ty", -3))
    sources(3, y_land.at[2], 0)
    sources(6, y_land.at[5], 0)
    for q in (3, 6):
        for i in range(4):
            choose(q, i)
        meet(q, 0, 0, 4)

    for e, way in ((0, -1), (1, 1)):
        copies.arrived(("z", way))
        parts = [z_land[e, c].astype(jnp.float32) for c in range(3)]
        for c in range(3):
            src[8 * PATCHES + e, c, pl.ds(PAD, N), :] = parts[c]
        src[8 * PATCHES + e, 3, pl.ds(PAD, N), :] = beta(parts)

        def one(w, carry, e=e):
            interact(OWN, meets[e], 8 * PATCHES + e, w)
            return carry

        lax.fori_loop(0, N // WINDOW, one, 0)

    for p in range(PATCHES):
        onward(3, 1, p)
    for p in range(PATCHES):
        for way in (2, -2):
            copies.arrived(("x", way, 1, p))
    for i in (TWO, RIGHT, LEFT):
        targets(i, 1)
    meet(0, 1, 0, OWN)

    copies.arrived(("ty", 4))
    for i in range(4):
        choose(7, i)

    def finish(k):
        wa, wb = CHUNKS[k][2]
        for p in range(PATCHES):
            for way in (4, -4):
                copies.arrived(("y", way, k, p))
        sources(7, y_land.at[6], k)
        meet(7, k, TWO, TWO + 1)
        pack(TWO, wa)
        copies.start(("raw", wa), ship.at[TWO, wa], raw.at[wa], right)
        pack(TWO, wb)
        copies.start(("raw", wb), ship.at[TWO, wb], raw.at[wb], left)
        meet(7, k, RIGHT, LEFT + 1)
        pack(RIGHT, wb)
        copies.start(("done", 0, wb), ship.at[RIGHT, wb], done.at[0, wb], right)
        pack(LEFT, wa)
        copies.start(("done", 1, wa), ship.at[LEFT, wa], done.at[1, wa], left)
        meet(7, k, OWN, OWN + 1)

    def relay(k):
        wa, wb = CHUNKS[k][2]
        copies.arrived(("raw", wa))
        pack(RIGHT, wa, raw.at[wa])
        copies.start(("done", 0, wa), ship.at[RIGHT, wa], done.at[0, wa], right)
        copies.arrived(("raw", wb))
        pack(LEFT, wb, raw.at[wb])
        copies.start(("done", 1, wb), ship.at[LEFT, wb], done.at[1, wb], left)

    def gather(k):
        for w in CHUNKS[k][2]:
            copies.arrived(("done", 0, w))
            copies.arrived(("done", 1, w))
            collect(w)

    finish(0)
    sources(1, y_land.at[0], 1)
    sources(4, y_land.at[3], 1)
    meet(1, 1, 0, 4)
    meet(4, 1, 0, 4)
    for p in range(PATCHES):
        onward(4, 1, p)
    relay(0)
    for q, slot in ((2, 1), (5, 4), (3, 2), (6, 5)):
        sources(q, y_land.at[slot], 1)
        meet(q, 1, 0, 4)
    finish(1)
    relay(1)
    gather(0)
    gather(1)

    for p in range(PATCHES):
        rows = pl.ds(p * N, N)
        for c in range(3):
            out[c, 0, rows, :] = out[c, 0, rows, :] + share[rows, :] * force[p, c].T
    copies.sent()


def shards(positions, velocity, node_mass, stiffness, contact_patch, cross_patch):
    table = contact_patch[0]
    cross = cross_patch[0]
    vmem, smem, far = pltpu.VMEM, pltpu.SMEM, pl.ANY
    f32, bf16, i32 = jnp.float32, jnp.bfloat16, jnp.int32
    windows = N // WINDOW
    return pl.pallas_call(
        kernel,
        out_shape=jax.ShapeDtypeStruct(velocity.shape, f32),
        in_specs=[pl.BlockSpec(memory_space=smem)] * 2 + [pl.BlockSpec(memory_space=far)] * 4,
        out_specs=pl.BlockSpec(memory_space=vmem),
        scratch_shapes=[
            vmem((3, ROWS + 2 * PAD, N), f32),
            vmem((ROWS, N), bf16),
            vmem((ROWS, N), bf16),
            vmem((ROWS + 2 * PAD, N), f32),
            vmem((ROWS, N), f32),
            vmem((PATCHES, 3, N, N), bf16),
            vmem((7, PATCHES, 3, N, N), bf16),
            vmem((3, PATCHES, 3, N, N), bf16),
            vmem((8 * PATCHES + 2, 4, N + 2 * PAD, N), f32),
            vmem((4 * PATCHES, 3, N, N), f32),
            vmem((4 * PATCHES, 4, N, N), f32),
            vmem((3, windows, PATCHES, 3, WINDOW, N), bf16),
            vmem((windows, PATCHES, 3, WINDOW, N), bf16),
            vmem((2, windows, PATCHES, 3, WINDOW, N), bf16),
            vmem((PATCHES, 3, N, N), f32),
            vmem((2, 3, N, N), bf16),
            vmem((2, 3, N, N), bf16),
            vmem((2, 8, N), f32),
            vmem((2, 8, N), f32),
        ]
        + [smem((1, RUNS), i32)] * 10
        + [
            smem((2, 32), i32),
            pltpu.SemaphoreType.DMA((6,)),
            pltpu.SemaphoreType.DMA((COPIES,)),
            pltpu.SemaphoreType.DMA((COPIES,)),
        ],
        compiler_params=pltpu.CompilerParams(
            collective_id=0, has_side_effects=True, vmem_limit_bytes=48 * 2**20
        ),
        cost_estimate=pl.CostEstimate(
            flops=600_000_000, bytes_accessed=2_000_000, transcendentals=40_000_000
        ),
    )(table, cross, positions, velocity, node_mass, stiffness)


def solution(mesh):
    return jax.shard_map(
        shards,
        mesh=mesh,
        in_specs=(
            P(None, "seg", "dev", None),
            P(None, "seg", "dev", None),
            P("seg", "dev", None),
            P("seg", "dev", None),
            P("seg", "dev", None),
            P("seg", "dev", None),
        ),
        out_specs=P(None, "seg", "dev", None),
        check_vma=False,
    )
```

```python
import functools
import math

import jax
import jax.numpy as jnp
from jax import lax
from jax.experimental import pallas as pl
from jax.experimental.pallas import tpu as pltpu
from jax.sharding import PartitionSpec as P

RUNS = 32
XS = 4
YS = 8
PATCHES = 3
N = 128
BAND = 4
PAD = 8
STRIDE = 4
WINDOW = 8 * STRIDE
ROWS = PATCHES * N

penalty = 1.5
reach_sq = 4.0
time_step = 0.2
K = math.log2(math.e) / reach_sq
FAR = -1.0e4

CHUNKS = (
    (0, 48, (0,)),
    (48, 80, (1,)),
    (80, 112, (2,)),
    (112, 128, (3,)),
)

HALVES = (
    ((0, 32), (32, 48)),
    ((48, 64), (64, 80)),
    ((80, 96), (96, 112)),
    ((112, 112), (112, 128)),
)

ORDER = (
    ('y', 1, 0),
    ('y', 1, 1),
    ('y', 1, 2),
    ('y', 1, 3),
    ('x', 1, 0),
    ('x', 1, 1),
    ('x', 1, 2),
    ('x', 1, 3),
    ('z',),
    ('h',),
    ('y', 2, 0),
    ('s', 1, 0),
    ('x', 2, 0),
    ('t', 1, 0),
    ('m', 0, 0, 1),
    ('m', 1, 0, 1),
    ('b',),
    ('y', 2, 1),
    ('x', 2, 1),
    ('s', 1, 1),
    ('t', 1, 1),
    ('m', 0, 1, 1),
    ('m', 1, 1, 1),
    ('y', 2, 2),
    ('x', 2, 2),
    ('t', 1, 2),
    ('y', 2, 3),
    ('s', 1, 2),
    ('s', 1, 3),
    ('m', 0, 2, 1),
    ('m', 1, 2, 1),
    ('x', 2, 3),
    ('t', 1, 3),
    ('m', 0, 3, 1),
    ('m', 1, 3, 1),
    ('t', 2, 0),
    ('m', 0, 0, 0),
    ('m', 1, 0, 0),
    ('w',),
    ('y', 3, 0),
    ('s', 2, 0),
    ('t', 2, 1),
    ('m', 2, 0, 2),
    ('y', 3, 1),
    ('s', 2, 1),
    ('t', 2, 2),
    ('t', 2, 3),
    ('m', 0, 1, 0),
    ('m', 1, 1, 0),
    ('m', 2, 1, 2),
    ('m', 0, 2, 0),
    ('m', 1, 2, 0),
    ('m', 0, 3, 0),
    ('y', 3, 2),
    ('s', 2, 2),
    ('m', 2, 2, 2),
    ('y', 3, 3),
    ('s', 2, 3),
    ('m', 1, 3, 0),
    ('m', 2, 3, 2),
    ('y', 4, 0),
    ('s', 3, 0),
    ('m', 3, 0, 2),
    ('y', 4, 1),
    ('s', 3, 1),
    ('m', 3, 1, 2),
    ('y', 4, 2),
    ('s', 3, 2),
    ('m', 3, 2, 2),
    ('y', 4, 3),
    ('s', 3, 3),
    ('m', 3, 3, 2),
    ('s', 4, 0),
    ('m', 4, 0, 0),
    ('r', 0, 0),
    ('m', 4, 0, 1),
    ('r', 1, 0),
    ('s', 4, 1),
    ('m', 4, 0, 3),
    ('m', 4, 1, 0),
    ('r', 0, 1),
    ('m', 4, 1, 1),
    ('r', 1, 1),
    ('s', 4, 2),
    ('m', 4, 1, 3),
    ('m', 4, 2, 0),
    ('r', 0, 2),
    ('s', 4, 3),
    ('m', 4, 2, 1),
    ('r', 1, 2),
    ('m', 4, 2, 3),
    ('m', 4, 3, 0),
    ('r', 0, 3),
    ('m', 4, 3, 1),
    ('r', 1, 3),
    ('m', 4, 3, 3),
    ('r', 2, 0),
    ('r', 2, 1),
    ('r', 2, 2),
    ('r', 2, 3),
    ('c', 0),
    ('c', 1),
    ('c', 2),
    ('c', 3),
)

TWO, RIGHT, LEFT, OWN = range(4)
MEET = {0: (TWO, TWO + 1), 1: (RIGHT, OWN + 1), 2: (TWO, OWN + 1), 3: (OWN, OWN + 1)}
COPIES = 160


class Copies:
    def __init__(self, send_sem, recv_sem):
        self.send_sem, self.recv_sem = send_sem, recv_sem
        self.made = {}
        self.seen = set()

    def start(self, name, src, dst, device):
        n = len(self.made)
        copy = pltpu.make_async_remote_copy(
            src_ref=src,
            dst_ref=dst,
            send_sem=self.send_sem.at[n],
            recv_sem=self.recv_sem.at[n],
            device_id=device,
            device_id_type=pl.DeviceIdType.MESH,
        )
        copy.start()
        self.made[name] = copy

    def arrived(self, *names):
        for name in names:
            if name in self.made and name not in self.seen:
                self.made[name].wait_recv()
                self.seen.add(name)

    def sent(self):
        for copy in self.made.values():
            copy.wait_send()


def kernel(
    contact, facing, pos, vel, mass, stiff, out,
    place, mass_v, stiff_v, spring, share, own, y_land, x_land, src, tgt, acc,
    ship, raw, done, force, z_send, z_land, h_send, h_land,
    tab_y1, tab_y2, tab_y3, tab_y4, tab_y5, tab_y6, tab_y7, tab_x1, tab_x2, tab_x3, table, cross, pick,
    local_sem, send_sem, recv_sem,
):
    seg = lax.axis_index("seg")
    dev = lax.axis_index("dev")
    segs = lax.axis_size("seg")
    y = dev // XS
    x = dev % XS

    def at(dy, dx):
        return (seg, lax.rem(y + dy, YS) * XS + lax.rem(x + dx, XS))

    up, down = at(1, 0), at(YS - 1, 0)
    right, left = at(0, 1), at(0, XS - 1)
    seg_next, seg_prev = (lax.rem(seg + 1, segs), dev), (lax.rem(seg + segs - 1, segs), dev)
    dev_next, dev_prev = (seg, lax.rem(dev + 1, RUNS)), (seg, lax.rem(dev + RUNS - 1, RUNS))

    barrier = pltpu.get_barrier_semaphore()
    peers = (up, down, right, left, seg_next, seg_prev, dev_next, dev_prev)
    for peer in peers:
        pl.semaphore_signal(barrier, inc=1, device_id=peer, device_id_type=pl.DeviceIdType.MESH)

    loads = []
    for p in range(PATCHES):
        loads.append(
            pltpu.make_async_copy(
                pos.at[:, 0, pl.ds(p * N, N), :],
                place.at[:, pl.ds(PAD + p * N, N), :],
                local_sem.at[p],
            )
        )
    loads.append(pltpu.make_async_copy(stiff.at[0], stiff_v, local_sem.at[3]))
    loads.append(pltpu.make_async_copy(mass.at[0], mass_v, local_sem.at[4]))
    loads.append(pltpu.make_async_copy(vel, out, local_sem.at[5]))
    loads.append(pltpu.make_async_copy(contact.at[0], table, local_sem.at[6]))
    loads.append(pltpu.make_async_copy(facing.at[0], cross, local_sem.at[7]))
    for load in loads:
        load.start()

    def clear(n, carry):
        for c in range(4):
            edge = jnp.full((PAD, N), FAR if c == 3 else 0.0, jnp.float32)
            src[n, c, pl.ds(0, PAD), :] = edge
            src[n, c, pl.ds(PAD + N, PAD), :] = edge
        return carry

    lax.fori_loop(0, 8 * PATCHES + 2, clear, 0)

    def clear_sums(n, carry):
        for c in range(4):
            acc[n, c] = jnp.zeros((N, N), jnp.float32)
        return carry

    copies = Copies(send_sem, recv_sem)

    def columns(k):
        lo, hi, _ = CHUNKS[k]
        return pl.ds(lo, hi - lo)

    def beta(xs):
        return -K * (xs[0] * xs[0] + xs[1] * xs[1] + xs[2] * xs[2])

    for p in range(PATCHES):
        loads[p].wait()
    for p in range(PATCHES):
        parts = []
        for c in range(3):
            turned = place[c, pl.ds(PAD + p * N, N), :].T.astype(jnp.bfloat16)
            own[p, c] = turned
            parts.append(turned.astype(jnp.float32))
        for c in range(3):
            src[p, c, pl.ds(PAD, N), :] = parts[c]
            tgt[OWN * PATCHES + p, c] = parts[c] * (2 * K)
        src[p, 3, pl.ds(PAD, N), :] = beta(parts)
    loads[3].wait()
    for e, row in enumerate((0, ROWS - 1)):
        first = row // 16 * 16
        for c in range(3):
            h_send[e, pl.ds(c, 1), :] = place[c, pl.ds(PAD + row, 1), :]
        edge = stiff_v[pl.ds(first, 16), :].astype(jnp.float32)
        h_send[e, pl.ds(3, 1), :] = edge[row - first : row - first + 1]
        h_send[e, pl.ds(4, 4), :] = jnp.zeros((4, N), jnp.float32)

    loads[6].wait()
    loads[7].wait()
    pl.semaphore_wait(barrier, len(peers))
    tabs_y = (table, tab_y1, tab_y2, tab_y3, tab_y4, tab_y5, tab_y6, tab_y7)
    copies.start(("ty", 1), table, tab_y1, up)
    copies.start(("ty", -1), table, tab_y4, down)
    copies.start(("tx", 1), table, tab_x3, right)
    copies.start(("tx", -1), table, tab_x2, left)
    copies.start(("h", -1), h_send.at[0], h_land.at[1], dev_prev)
    copies.start(("h", 1), h_send.at[1], h_land.at[0], dev_next)

    def interact(i, ia, sb, w):
        sa = i * PATCHES + jnp.maximum(ia, 0)
        base = w * WINDOW
        seen = {}

        def b(j, c):
            if (j, c) not in seen:
                seen[j, c] = src[sb, c, pl.ds(base + (PAD + j), 8, stride=STRIDE), :]
            return seen[j, c]

        for u in range(STRIDE):
            a = [tgt[sa, c, pl.ds(base + u, 8, stride=STRIDE), :] for c in range(3)]
            sums = [None] * 4
            for t in range(-BAND, BAND + 1):
                bs = [b(u + t, c) for c in range(4)]
                w_ = jnp.exp2((a[0] * bs[0] + a[1] * bs[1]) + (a[2] * bs[2] + bs[3]))
                terms = [w_ * bs[0], w_ * bs[1], w_ * bs[2], w_]
                sums = [g if s is None else s + g for s, g in zip(sums, terms)]
            rows = pl.ds(pl.multiple_of(base + u * 8, 8), 8)
            for p in range(PATCHES):
                for c in range(4):
                    acc[i * PATCHES + p, c, rows, :] += jnp.where(ia == p, sums[c], 0.0)

    def sources(q, land, k):
        lo, hi, _ = CHUNKS[k]

        def one(p, carry):
            parts = [land[p, c, pl.ds(lo, hi - lo), :].astype(jnp.float32) for c in range(3)]
            for c in range(3):
                src[q * PATCHES + p, c, pl.ds(PAD + lo, hi - lo), :] = parts[c]
            src[q * PATCHES + p, 3, pl.ds(PAD + lo, hi - lo), :] = beta(parts)
            return carry

        lax.fori_loop(0, PATCHES, one, 0)

    def targets(i, k):
        lo, hi, _ = CHUNKS[k]

        def one(p, carry):
            for c in range(3):
                part = x_land[i, p, c, pl.ds(lo, hi - lo), :].astype(jnp.float32)
                tgt[i * PATCHES + p, c, pl.ds(lo, hi - lo), :] = part * (2 * K)
            return carry

        lax.fori_loop(0, PATCHES, one, 0)

    tabs_x = (tab_x1, tab_x2, tab_x3, table)
    run_y = [lax.rem(y + d, YS) for d in (0, 7, 6, 5, 1, 2, 3, 4)]
    run_x = [lax.rem(x + d, XS) for d in (2, 1, 3, 0)]

    def choose(q, i):
        pick[0, q * 4 + i] = tabs_x[i][0, run_y[q] * XS + x]
        pick[1, q * 4 + i] = q * PATCHES + jnp.maximum(tabs_y[q][0, y * XS + run_x[i]], 0)

    def meet(q, runs, k, group):
        first, last = MEET[group]
        if group == 1 and q in (0, 7):
            last = OWN
        windows = CHUNKS[k][2]
        for n in range(runs):
            for i in range(first, last):
                choose(q + 3 * n, i)

        def one(n, carry):
            i = first + n // len(windows) % (last - first)
            at_q = q + 3 * (n // (len(windows) * (last - first)))
            interact(i, pick[0, at_q * 4 + i], pick[1, at_q * 4 + i], windows[0] + n % len(windows))
            return carry

        lax.fori_loop(0, runs * (last - first) * len(windows), one, 0)

    def reduced(i, w, u, p):
        rows = pl.ds(w * WINDOW + u * 8, 8)
        a = [tgt[i * PATCHES + p, c, pl.ds(w * WINDOW + u, 8, stride=STRIDE), :] for c in range(3)]
        level = penalty * jnp.exp2((a[0] * a[0] + a[1] * a[1] + a[2] * a[2]) * (-0.25 / K))
        whole = acc[i * PATCHES + p, 3, rows, :] * (0.5 / K)
        return [level * (a[c] * whole - acc[i * PATCHES + p, c, rows, :]) for c in range(3)]

    def pack(i, w, h, extra=None):
        def one(p, carry):
            pair = [reduced(i, w, 2 * h + e, p) for e in range(2)]
            for c in range(3):
                f = jnp.concatenate([pair[0][c], pair[1][c]], axis=0)
                if extra is not None:
                    f = f + extra[p, c].astype(jnp.float32)
                ship[i, w, h, p, c] = f.astype(jnp.bfloat16)
            return carry

        lax.fori_loop(0, PATCHES, one, 0)

    def collect(w):
        def one(p, carry):
            for h in range(STRIDE // 2):
                pair = [reduced(OWN, w, 2 * h + e, p) for e in range(2)]
                for c in range(3):
                    f = jnp.concatenate([pair[0][c], pair[1][c]], axis=0)
                    f = f + done[0, w, h, p, c].astype(jnp.float32)
                    f = f + done[1, w, h, p, c].astype(jnp.float32)
                    for e in range(2):
                        at_rows = pl.ds(w * WINDOW + 2 * h + e, 8, stride=STRIDE)
                        force[p, c, at_rows, :] = f[e * 8 : e * 8 + 8]
            return carry

        lax.fori_loop(0, PATCHES, one, 0)

    ways = ((1, 0, up), (-1, 3, down))

    def along(d, k):
        for way, slot, peer in ways:
            copies.arrived(("y", way * (d - 1), k))
            lo, hi, _ = CHUNKS[k]
            if d == 4:
                lo, hi = HALVES[k][0 if way == 1 else 1]
            if lo == hi:
                continue
            cols = pl.ds(lo, hi - lo)
            to = 6 if d == 4 else slot + d - 1
            part = own.at[:, :, cols, :] if d == 1 else y_land.at[slot + d - 2, :, :, cols, :]
            copies.start(("y", way * d, k), part, y_land.at[to, :, :, cols, :], peer)
        if k == 0 and d > 1:
            for way, slot, peer in ways[: 1 if d == 4 else 2]:
                copies.arrived(("ty", way * (d - 1)))
                to = 7 if d == 4 else slot + d
                copies.start(("ty", way * d), tabs_y[slot + d - 1], tabs_y[to], peer)

    def across(d, k):
        for n, (way, slot, peer) in enumerate(((1, LEFT, right), (-1, RIGHT, left))):
            lo, hi, _ = CHUNKS[k]
            if d == 2:
                copies.arrived(("x", way, k))
                lo, hi = HALVES[k][n]
            if lo == hi:
                continue
            cols = pl.ds(lo, hi - lo)
            part = own.at[:, :, cols, :] if d == 1 else x_land.at[slot, :, :, cols, :]
            to = slot if d == 1 else TWO
            copies.start(("x", way * d, k), part, x_land.at[to, :, :, cols, :], peer)
        if k == 0 and d == 2:
            copies.arrived(("tx", 1))
            copies.start(("tx", 2), tab_x3, tab_x1, right)

    def reduce_stage(stage, k):
        for w in CHUNKS[k][2]:
            for h, i, peer in ((0, RIGHT, right), (1, LEFT, left)):
                if stage == 0:
                    pack(TWO, w, h)
                    copies.start(("raw", w, h), ship.at[TWO, w, h], raw.at[w, h], peer)
                elif stage == 1:
                    pack(i, w, 1 - h)
                    copies.start(("done", w, h, 1 - h), ship.at[i, w, 1 - h], done.at[h, w, 1 - h], peer)
                else:
                    copies.arrived(("raw", w, h))
                    pack(i, w, h, raw.at[w, h])
                    copies.start(("done", w, h, h), ship.at[i, w, h], done.at[h, w, h], peer)

    def base_rows(b, carry):
        r = pl.multiple_of(b * 16, 16)
        lane = lax.broadcasted_iota(jnp.int32, (16, N), 1)
        after = jnp.where(lane == N - 1, 0.0, 0.5)
        before = jnp.where(lane == 0, 0.0, 0.5)
        s = spring[pl.ds(PAD + r, 16), :]
        s_up = 0.5 * (s + spring[pl.ds(PAD + r - 1, 16), :])
        s_down = 0.5 * (s + spring[pl.ds(PAD + r + 1, 16), :])
        s_after = after * (s + pltpu.roll(s, N - 1, 1))
        s_before = before * (s + pltpu.roll(s, 1, 1))
        part = time_step / mass_v[pl.ds(r, 16), :].astype(jnp.float32)
        share[pl.ds(r, 16), :] = part
        for c in range(3):
            v = place[c, pl.ds(PAD + r, 16), :]
            f = s_up * (place[c, pl.ds(PAD + r - 1, 16), :] - v)
            f = f + s_down * (place[c, pl.ds(PAD + r + 1, 16), :] - v)
            f = f + s_after * (pltpu.roll(v, N - 1, 1) - v)
            f = f + s_before * (pltpu.roll(v, 1, 1) - v)
            out[c, 0, pl.ds(r, 16), :] = out[c, 0, pl.ds(r, 16), :] + part * f
        return carry

    def halo():
        for b in range(ROWS // WINDOW):
            rows = pl.ds(b * WINDOW, WINDOW)
            spring[pl.ds(PAD + b * WINDOW, WINDOW), :] = stiff_v[rows, :].astype(jnp.float32)
        copies.arrived(("h", -1), ("h", 1))
        for e, row, edge, last in ((0, PAD - 1, PAD, 0), (1, PAD + ROWS, PAD + ROWS - 1, RUNS - 1)):
            for c in range(3):
                place[c, pl.ds(row, 1), :] = jnp.where(
                    dev == last, place[c, pl.ds(edge, 1), :], h_land[e, pl.ds(c, 1), :]
                )
            spring[pl.ds(row, 1), :] = h_land[e, pl.ds(3, 1), :]
        loads[4].wait()
        loads[5].wait()
        lax.fori_loop(0, ROWS // 16, base_rows, 0)

    meets = [cross[0, 0], cross[0, 1]]

    def send_cross():
        for c in range(3):
            z_send[0, c] = own[meets[0], c]
            z_send[1, c] = own[meets[1], c]
        copies.start(("z", 1), z_send.at[0], z_land.at[1], seg_next)
        copies.start(("z", -1), z_send.at[1], z_land.at[0], seg_prev)

    def meet_cross():
        for e, way in ((0, -1), (1, 1)):
            copies.arrived(("z", way))
            parts = [z_land[e, c].astype(jnp.float32) for c in range(3)]
            for c in range(3):
                src[8 * PATCHES + e, c, pl.ds(PAD, N), :] = parts[c]
            src[8 * PATCHES + e, 3, pl.ds(PAD, N), :] = beta(parts)

        def one(n, carry):
            e = n // (N // WINDOW)
            ia = jnp.where(e == 0, meets[0], meets[1])
            interact(OWN, ia, 8 * PATCHES + e, n % (N // WINDOW))
            return carry

        lax.fori_loop(0, 2 * N // WINDOW, one, 0)

    for kind, *step in ORDER:
        if kind == "y":
            along(*step)
        elif kind == "x":
            across(*step)
        elif kind == "t":
            way, k = step
            if way == 1:
                copies.arrived(("x", 1, k), ("x", -1, k))
                targets(RIGHT, k)
                targets(LEFT, k)
            else:
                copies.arrived(("x", 2, k), ("x", -2, k))
                targets(TWO, k)
        elif kind == "s":
            d, k = step
            copies.arrived(("y", d, k), ("y", -d, k))
            if d == 4:
                sources(7, y_land.at[6], k)
            else:
                sources(d, y_land.at[d - 1], k)
                sources(d + 3, y_land.at[d + 2], k)
        elif kind == "m":
            d, k, group = step
            if k == 0:
                copies.arrived(("ty", d), ("ty", -d), ("tx", 1), ("tx", -1))
                if group in (0, 2):
                    copies.arrived(("tx", 2))
            meet(7 if d == 4 else d, 1 if d in (0, 4) else 2, k, group)
        elif kind == "r":
            reduce_stage(*step)
        elif kind == "c":
            (k,) = step
            for w in CHUNKS[k][2]:
                copies.arrived(*((("done", w, h, e)) for h in range(2) for e in range(2)))
                collect(w)
        elif kind == "h":
            lax.fori_loop(0, 4 * PATCHES, clear_sums, 0)
        elif kind == "b":
            halo()
        elif kind == "z":
            send_cross()
        elif kind == "w":
            meet_cross()

    for p in range(PATCHES):
        rows = pl.ds(p * N, N)
        for c in range(3):
            out[c, 0, rows, :] = out[c, 0, rows, :] + share[rows, :] * force[p, c].T
    copies.sent()


def shards(positions, velocity, node_mass, stiffness, contact_patch, cross_patch):
    vmem, smem = pltpu.VMEM, pltpu.SMEM
    f32, bf16, i32 = jnp.float32, jnp.bfloat16, jnp.int32
    windows = N // WINDOW
    return pl.pallas_call(
        kernel,
        out_shape=jax.ShapeDtypeStruct(velocity.shape, f32),
        in_specs=[pl.BlockSpec(memory_space=pltpu.HBM)] * 6,
        out_specs=pl.BlockSpec(memory_space=vmem),
        scratch_shapes=[
            vmem((3, ROWS + 2 * PAD, N), f32),
            vmem((ROWS, N), bf16),
            vmem((ROWS, N), bf16),
            vmem((ROWS + 2 * PAD, N), f32),
            vmem((ROWS, N), f32),
            vmem((PATCHES, 3, N, N), bf16),
            vmem((7, PATCHES, 3, N, N), bf16),
            vmem((3, PATCHES, 3, N, N), bf16),
            vmem((8 * PATCHES + 2, 4, N + 2 * PAD, N), f32),
            vmem((4 * PATCHES, 3, N, N), f32),
            vmem((4 * PATCHES, 4, N, N), f32),
            vmem((3, windows, 2, PATCHES, 3, WINDOW // 2, N), bf16),
            vmem((windows, 2, PATCHES, 3, WINDOW // 2, N), bf16),
            vmem((2, windows, 2, PATCHES, 3, WINDOW // 2, N), bf16),
            vmem((PATCHES, 3, N, N), f32),
            vmem((2, 3, N, N), bf16),
            vmem((2, 3, N, N), bf16),
            vmem((2, 8, N), f32),
            vmem((2, 8, N), f32),
        ]
        + [smem((1, RUNS), i32)] * 11
        + [
            smem((1, 2), i32),
            smem((2, 32), i32),
            pltpu.SemaphoreType.DMA((8,)),
            pltpu.SemaphoreType.DMA((COPIES,)),
            pltpu.SemaphoreType.DMA((COPIES,)),
        ],
        compiler_params=pltpu.CompilerParams(
            collective_id=0, has_side_effects=True, vmem_limit_bytes=60 * 2**20
        ),
        cost_estimate=pl.CostEstimate(
            flops=600_000_000, bytes_accessed=2_000_000, transcendentals=40_000_000
        ),
    )(contact_patch, cross_patch, positions, velocity, node_mass, stiffness)


def solution(mesh):
    return jax.shard_map(
        shards,
        mesh=mesh,
        in_specs=(
            P(None, "seg", "dev", None),
            P(None, "seg", "dev", None),
            P("seg", "dev", None),
            P("seg", "dev", None),
            P("seg", "dev", None),
            P("seg", "dev", None),
        ),
        out_specs=P(None, "seg", "dev", None),
        check_vma=False,
    )
```
